32 devices in a mesh: ctx: 8 (over z, x), wsh: 4 (over y, core).
Axes of the slice: x: 2, y: 2, z: 4, core: 2. Of those that a mesh axis runs over, the one named last changes fastest.
Arguments:
- tokens: bfloat16 [4, 2048, 1024], P('wsh', 'ctx'), may hold values from -6 to 6
- block_map: int32 [8, 2], replicated, may hold values from 0 to 15, as said below
- positions: int32 [4, 2048], P('wsh'), may hold values from 0 to 255, as said below
- norm_gain_one: bfloat16 [1024], P('wsh'), may hold values from 0.5 to 1.5
- norm_shift_one: bfloat16 [1024], P('wsh'), may hold values from -2.5 to 2.5
- qkv_weight: bfloat16 [1024, 3072], P('wsh'), may hold values from -0.1875 to 0.1875
- query_bias: bfloat16 [1024], P('wsh'), may hold values from -2.5 to 2.5
- value_bias: bfloat16 [1024], P('wsh'), may hold values from -2.5 to 2.5
- dense_weight: bfloat16 [1024, 1024], P('wsh'), may hold values from -0.5 to 0.5
- dense_bias: bfloat16 [1024], P('wsh'), may hold values from -2.5 to 2.5
- norm_gain_two: bfloat16 [1024], P('wsh'), may hold values from 0.5 to 1.5
- norm_shift_two: bfloat16 [1024], P('wsh'), may hold values from -2.5 to 2.5
- up_weight: bfloat16 [1024, 4096], P('wsh'), may hold values from -0.1875 to 0.1875
- up_bias: bfloat16 [4096], P('wsh'), may hold values from -2.5 to 2.5
- down_weight: bfloat16 [4096, 1024], P('wsh'), may hold values from -0.09375 to 0.09375
- down_bias: bfloat16 [1024], P('wsh'), may hold values from -2.5 to 2.5
- cotangent: bfloat16 [4, 2048, 1024], P('wsh', 'ctx'), may hold values from -6 to 6
Outputs:
- layer_out: bfloat16 [4, 2048, 1024], P('wsh', 'ctx')
- input_grad: bfloat16 [4, 2048, 1024], P('wsh', 'ctx')
- grad_norm_gain_one: float32 [1024], P('wsh')
- grad_norm_shift_one: float32 [1024], P('wsh')
- grad_qkv_weight: float32 [1024, 3072], P('wsh')
- grad_query_bias: float32 [1024], P('wsh')
- grad_value_bias: float32 [1024], P('wsh')
- grad_dense_weight: float32 [1024, 1024], P('wsh')
- grad_dense_bias: float32 [1024], P('wsh')
- grad_norm_gain_two: float32 [1024], P('wsh')
- grad_norm_shift_two: float32 [1024], P('wsh')
- grad_up_weight: float32 [1024, 4096], P('wsh')
- grad_up_bias: float32 [4096], P('wsh')
- grad_down_weight: float32 [4096, 1024], P('wsh')
- grad_down_bias: float32 [1024], P('wsh')
The draws below stay inside these ranges and needn't reach their ends.
Inputs may be any that keep to these rules, and one draw needn't show every extreme that they name: `block_map`: row i lists, in stored order, the blocks b and 15 - b for one b < 8; every block appears exactly once. Each sequence's positions start at 0 and never fall; from one token to the next they rise by 0 or 1, by 1 at exactly (2047) // 8 of the steps.
All inputs are finite; a program needn't handle non-finite values.
Results may differ from the reference program's by a relative error of at most 0.02.
Values may be sent and summed in bfloat16 or wider, within the bound.
A program may use at most 320 MiB of HBM per device.

```python
import math
import jax
import jax.numpy as jnp
from jax import lax

D = 1024
HEADS = 16
HEAD_DIM = 64
FF = 4096
TOK_DEV = 256
HALF = 128
LENGTH = 2048
SEQS = 4
N_CTX = 8


def draw_block_map(key, part):
    key = jax.random.fold_in(key, 11)
    offset_key, flip_key = jax.random.split(key)
    shift_amount = jax.random.randint(offset_key, (), 0, N_CTX)
    flip_bits = jax.random.randint(flip_key, (N_CTX,), 0, 2)
    device_ids = jnp.arange(N_CTX, dtype=jnp.int32)
    offset = (device_ids - shift_amount) % N_CTX
    pair_index = jnp.where(offset < N_CTX // 2, 2 * offset, 2 * (offset - N_CTX // 2) + 1)
    late_block = 2 * N_CTX - 1 - pair_index
    first_slot = jnp.where(flip_bits == 1, late_block, pair_index)
    second_slot = jnp.where(flip_bits == 1, pair_index, late_block)
    return jnp.stack([first_slot, second_slot], axis=1).astype(jnp.int32)


def draw_positions(key, part):
    key = jax.random.fold_in(key, 23)
    step_count = LENGTH - 1
    pattern = (jnp.arange(step_count, dtype=jnp.int32) < step_count // 8).astype(jnp.int32)
    seq_keys = jax.random.split(key, SEQS)
    increments = jax.vmap(lambda one_key: jax.random.permutation(one_key, pattern))(seq_keys)
    summed = jnp.cumsum(increments, axis=1).astype(jnp.int32)
    starts = jnp.zeros((SEQS, 1), jnp.int32)
    return jnp.concatenate([starts, summed], axis=1).astype(jnp.int32)


def level_of(own_key, dims, shards, least, largest):
    level, own = 1.0, jax.random.fold_in(own_key, 6)
    for axis_at, parts in shards:
        steps = jnp.exp(jax.random.uniform(jax.random.fold_in(own, axis_at), (parts,), jnp.float32, least / len(shards), largest / len(shards)))
        level = level * jnp.repeat(steps, dims[axis_at] // parts).reshape([-1 if axis == axis_at else 1 for axis in range(len(dims))])
    return level


def scatter_about(own_key, extent, scale, limit, shards=(), kind=jnp.bfloat16):
    array = jax.random.normal(own_key, extent, jnp.float32) * scale
    if len(shards) > 0:
        array = level_of(own_key, extent, shards, -0.22, 0.18) * array
    return jnp.clip(array, min=-limit, max=limit).astype(kind)


def setup_inputs(seed: int = 0) -> dict:
    seeds = jax.random.split(jax.random.key(seed), 18)
    return {
        "tokens": scatter_about(seeds[0], (SEQS, LENGTH, D), 1.0, 6.0, ((0, 4), (1, 8))),
        "block_map": draw_block_map(jax.random.fold_in(seeds[17], 71), 0),
        "positions": draw_positions(jax.random.fold_in(seeds[17], 71), 0),
        "norm_gain_one": jnp.clip(1.0 + 0.1 * jax.random.normal(seeds[3], (D,), jnp.float32), 0.5, 1.5).astype(jnp.bfloat16),
        "norm_shift_one": scatter_about(seeds[4], (D,), 0.3, 2.5, ((0, 4),)),
        "qkv_weight": scatter_about(seeds[5], (D, 3 * D), D ** -0.5, 0.1875, ((0, 4),)),
        "query_bias": scatter_about(seeds[6], (D,), 0.3, 2.5, ((0, 4),)),
        "value_bias": scatter_about(seeds[7], (D,), 0.3, 2.5, ((0, 4),)),
        "dense_weight": scatter_about(seeds[8], (D, D), (D // 8) ** -0.5, 0.5, ((0, 4),)),
        "dense_bias": scatter_about(seeds[9], (D,), 0.3, 2.5, ((0, 4),)),
        "norm_gain_two": jnp.clip(1.0 + 0.1 * jax.random.normal(seeds[10], (D,), jnp.float32), 0.5, 1.5).astype(jnp.bfloat16),
        "norm_shift_two": scatter_about(seeds[11], (D,), 0.3, 2.5, ((0, 4),)),
        "up_weight": scatter_about(seeds[12], (D, FF), D ** -0.5, 0.1875, ((0, 4),)),
        "up_bias": scatter_about(seeds[13], (FF,), 0.3, 2.5, ((0, 4),)),
        "down_weight": scatter_about(seeds[14], (FF, D), FF ** -0.5, 0.09375, ((0, 4),)),
        "down_bias": scatter_about(seeds[15], (D,), 0.3, 2.5, ((0, 4),)),
        "cotangent": scatter_about(seeds[16], (SEQS, LENGTH, D), 1.0, 6.0, ((0, 4), (1, 8))),
    }


EPS = 1e-05
HIGHEST = lax.Precision.HIGHEST

@jax.custom_vjp
def low(v):
    return lax.optimization_barrier(v.astype(jnp.bfloat16)).astype(jnp.float32)

@jax.custom_vjp
def low_back(v):
    return v

def low_keep(v):
    return (low(v), None)

def low_pass(kept, grad):
    return (grad,)

def back_keep(v):
    return (v, None)

def back_low(kept, grad):
    return (low(grad),)
low.defvjp(low_keep, low_pass)
low_back.defvjp(back_keep, back_low)

def head_slopes(count):
    return 2.0 ** (-8.0 * (jnp.arange(count, dtype=jnp.float32) + 1.0) / count)

def layer_norm(values, gain_vec, shift_vec):
    row_mean = lax.optimization_barrier(jnp.mean(values, axis=-1, keepdims=True))
    centered = values - row_mean
    variance = lax.optimization_barrier(jnp.mean(centered * centered, axis=-1, keepdims=True))
    return centered * lax.rsqrt(variance + EPS) * gain_vec + shift_vec

def attention(query, keys, values, seq_pos):
    slopes = head_slopes(HEADS)
    score_scale = HEAD_DIM ** (-0.5)
    query_rows = math.gcd(512, LENGTH)
    block_count = LENGTH // query_rows
    key_heads = keys.reshape(LENGTH, HEADS, HEAD_DIM)
    value_heads = values.reshape(LENGTH, HEADS, HEAD_DIM)

    def one_block(block_items):
        query_block, pos_block = block_items
        raw_scores = low_back(jnp.einsum('qhd,khd->hqk', query_block, key_heads, precision=HIGHEST))
        distance = (pos_block[:, None] - seq_pos[None, :]).astype(jnp.float32)
        scores = raw_scores * score_scale - slopes[:, None, None] * distance[None]
        scores = jnp.where((distance >= 0.0)[None], scores, -jnp.inf)
        row_top = lax.optimization_barrier(jnp.max(scores, axis=-1, keepdims=True))
        exponents = jnp.exp(scores - row_top)
        weights = low(exponents / lax.optimization_barrier(jnp.sum(exponents, axis=-1, keepdims=True)))
        mixed = jnp.einsum('hqk,khd->qhd', weights, value_heads, precision=HIGHEST)
        return mixed.reshape(query_rows, D)
    blocks = lax.map(jax.checkpoint(one_block), (query.reshape(block_count, query_rows, HEADS, HEAD_DIM), seq_pos.reshape(block_count, query_rows)))
    return blocks.reshape(LENGTH, D)

def forward_one(params, inputs, seq_pos):
    gain_one, shift_one, qkv_full, query_shift, value_shift, dense_full, dense_shift, gain_two, shift_two, up_full, up_shift, down_full, down_shift = params
    normed = low(layer_norm(inputs, gain_one, shift_one))
    mixed = jnp.dot(normed, qkv_full, precision=HIGHEST)
    query = low_back(low(mixed[:, :D] + query_shift))
    keys = low_back(low(mixed[:, D:2 * D]))
    values = low_back(low(mixed[:, 2 * D:] + value_shift))
    attended = attention(query, keys, values, seq_pos)
    context = low_back(low(attended))
    projected = low_back(jnp.dot(context, dense_full, precision=HIGHEST) + dense_shift)
    middle = inputs + projected
    normed_two = low(layer_norm(middle, gain_two, shift_two))
    hidden = low_back(jnp.dot(normed_two, up_full, precision=HIGHEST) + up_shift)
    active = low(jax.nn.gelu(hidden, approximate=True))
    branch = low_back(jnp.dot(active, down_full, precision=HIGHEST) + down_shift)
    return middle + branch

def reference(tokens, block_map, positions, norm_gain_one, norm_shift_one, qkv_weight, query_bias, value_bias, dense_weight, dense_bias, norm_gain_two, norm_shift_two, up_weight, up_bias, down_weight, down_bias, cotangent):
    row_ids = jnp.arange(LENGTH, dtype=jnp.int32)
    stored_blocks = block_map[row_ids // TOK_DEV, row_ids // HALF % 2]
    seq_index = (stored_blocks * HALF + row_ids % HALF).astype(jnp.int32)
    params = tuple((item.astype(jnp.float32) for item in (norm_gain_one, norm_shift_one, qkv_weight, query_bias, value_bias, dense_weight, dense_bias, norm_gain_two, norm_shift_two, up_weight, up_bias, down_weight, down_bias)))

    def one_sequence(running, seq_items):
        seq_tokens, seq_positions, seq_cotangent = seq_items
        seq_pos = seq_positions[seq_index]
        result, pullback = jax.vjp(lambda prm, inputs: forward_one(prm, inputs, seq_pos), params, seq_tokens.astype(jnp.float32))
        gradients, grad_inputs = pullback(seq_cotangent.astype(jnp.float32))
        running = jax.tree.map(jnp.add, running, gradients)
        return (running, (result.astype(jnp.bfloat16), grad_inputs.astype(jnp.bfloat16)))
    start = tuple((jnp.zeros(item.shape, jnp.float32) for item in params))
    totals, (outputs, grad_inputs) = lax.scan(one_sequence, start, (tokens, positions, cotangent))
    return (outputs, grad_inputs) + tuple(totals)
```

```python
import functools

import jax
import jax.numpy as jnp
from jax import lax
from jax.experimental import pallas as pl
from jax.experimental.pallas import tpu as pltpu
from jax.sharding import PartitionSpec as P

HEADS = 16
EPS = 1e-05
LANES = 128
QUERY_TILE = 256
KEY_TILE = 512
FAR = -1e30
F32 = jnp.float32
BF16 = jnp.bfloat16


def norm_forward(values, gain_vec, shift_vec):
    row_mean = jnp.mean(values, axis=-1, keepdims=True)
    centered = values - row_mean
    variance = jnp.mean(centered * centered, axis=-1, keepdims=True)
    inverse = lax.rsqrt(variance + EPS)
    scaled = centered * inverse
    return (scaled * gain_vec + shift_vec, scaled, inverse)


def norm_backward(grad_out, scaled, inverse, gain_vec):
    grad_scaled = grad_out * gain_vec
    mean_grad = jnp.mean(grad_scaled, axis=-1, keepdims=True)
    mean_along = jnp.mean(grad_scaled * scaled, axis=-1, keepdims=True)
    grad_in = inverse * (grad_scaled - mean_grad - scaled * mean_along)
    return (grad_in, jnp.sum(grad_out * scaled, axis=0), jnp.sum(grad_out, axis=0))


def gelu_tanh(values):
    return jax.nn.gelu(values, approximate=True)


def dot(a, b, dims):
    return lax.dot_general(a, b, (dims, ((), ())), preferred_element_type=F32)


def column_sum(values):
    return jnp.sum(values.astype(F32), axis=0)


def slot_rows(order_ref, step, rows, first):
    slot = order_ref[step]
    src = slot // 2
    return src, pl.ds(pl.multiple_of(first + (slot % 2) * rows, 16), rows)


def split_heads(tile):
    lane = lax.broadcasted_iota(jnp.int32, tile.shape, 1)
    zero = jnp.zeros_like(tile)
    half = LANES // 2
    return (jnp.where(lane < half, tile, zero), jnp.where(lane >= half, tile, zero))


def load_sequence(query_block, half_tok, order_ref, packed_ref, q_s, k_s, v_s):
    first_key = 2 * query_block
    first_value = first_key + 2 * half_tok

    def load(step, _):
        src, rows = slot_rows(order_ref, step, query_block, 0)
        to = pl.ds(pl.multiple_of(step * query_block, 16), query_block)
        q_s[to, :] = packed_ref[src, rows, :]
        to = pl.ds(pl.multiple_of(step * half_tok, 16), half_tok)
        src, rows = slot_rows(order_ref, step, half_tok, first_key)
        k_s[to, :] = packed_ref[src, rows, :]
        src, rows = slot_rows(order_ref, step, half_tok, first_value)
        v_s[to, :] = packed_ref[src, rows, :]
        return 0

    lax.fori_loop(0, order_ref.shape[0], load, 0)


def transpose_into(to_ref, from_ref, key_tile):
    def turn(step, _):
        rows = pl.ds(pl.multiple_of(step * key_tile, key_tile), key_tile)
        to_ref[:, rows] = from_ref[rows, :].astype(F32).T.astype(BF16)
        return 0

    lax.fori_loop(0, from_ref.shape[0] // key_tile, turn, 0)


def tile_bias(key_pos_ref, keys, query_pos):
    distance = key_pos_ref[keys, :] - query_pos
    return jnp.where(distance <= 0.0, distance, FAR)


def forward_kernel(
    query_block, half_tok, query_tile, key_tile,
    order_ref, count_ref, slope_ref, packed_ref, query_pos_ref, key_pos_ref,
    context_ref, attended_ref, log_ref, q_s, k_s, v_s, vt_s,
):
    load_sequence(query_block, half_tok, order_ref, packed_ref, q_s, k_s, v_s)
    transpose_into(vt_s, v_s, key_tile)
    half = LANES // 2

    def query_step(qi, _):
        queries = pl.ds(pl.multiple_of(qi * query_tile, query_tile), query_tile)
        q_parts = split_heads(q_s[queries, :] * 0.125)
        query_pos = query_pos_ref[:, queries]

        def key_step(kj, carry):
            keys = pl.ds(pl.multiple_of(kj * key_tile, key_tile), key_tile)
            k_tile = k_s[keys, :]
            bias = tile_bias(key_pos_ref, keys, query_pos)
            out = []
            for h in range(2):
                top, total, acc = carry[h]
                scores = dot(k_tile, q_parts[h], ((1,), (1,))) + slope_ref[h] * bias
                new_top = jnp.maximum(top, jnp.max(scores, axis=0, keepdims=True))
                rescale = jnp.exp(top - new_top)
                weights = jnp.exp(scores - new_top)
                total = total * rescale + jnp.sum(weights, axis=0, keepdims=True)
                v_tile = vt_s[h * half : (h + 1) * half, keys]
                acc = acc * rescale + dot(v_tile, weights.astype(BF16), ((1,), (0,)))
                out.append((new_top, total, acc))
            return tuple(out)

        row = jnp.zeros((1, query_tile), F32)
        start = (row + FAR, row, jnp.zeros((half, query_tile), F32))
        ends = lax.fori_loop(0, count_ref[qi], key_step, (start, start))
        for h in range(2):
            top, total, acc = ends[h]
            attended_ref[h * half : (h + 1) * half, queries] = acc / total
            log_ref[h : h + 1, queries] = top + jnp.log(total)
        q_s[queries, :] = attended_ref[:, queries].T.astype(BF16)
        return 0

    lax.fori_loop(0, q_s.shape[0] // query_tile, query_step, 0)

    def put(step, _):
        src, rows = slot_rows(order_ref, step, query_block, 0)
        at = pl.ds(pl.multiple_of(step * query_block, 16), query_block)
        context_ref[src, rows, :] = q_s[at, :]
        return 0

    lax.fori_loop(0, order_ref.shape[0], put, 0)


def backward_kernel(
    query_block, half_tok, query_tile, key_tile,
    order_ref, count_ref, slope_ref, packed_ref, query_pos_ref, key_pos_ref,
    attended_ref, log_ref, grad_ref,
    out_ref, q_s, k_s, v_s, kt_s, g_s, gk_s, gv_s,
):
    load_sequence(query_block, half_tok, order_ref, packed_ref, q_s, k_s, v_s)
    transpose_into(kt_s, k_s, key_tile)
    half = LANES // 2

    def load(step, _):
        src, rows = slot_rows(order_ref, step, query_block, 0)
        at = pl.ds(pl.multiple_of(step * query_block, 16), query_block)
        g_s[at, :] = grad_ref[src, rows, :]
        return 0

    lax.fori_loop(0, order_ref.shape[0], load, 0)
    gk_s[...] = jnp.zeros_like(gk_s)
    gv_s[...] = jnp.zeros_like(gv_s)

    def query_step(qi, _):
        queries = pl.ds(pl.multiple_of(qi * query_tile, query_tile), query_tile)
        q_parts = split_heads(q_s[queries, :] * 0.125)
        g_tile = g_s[queries, :]
        g_parts = split_heads(g_tile)
        along = g_tile.astype(F32).T * attended_ref[:, queries]
        deltas = [
            jnp.sum(along[h * half : (h + 1) * half], axis=0, keepdims=True) for h in range(2)
        ]
        query_pos = query_pos_ref[:, queries]

        def key_step(kj, carry):
            keys = pl.ds(pl.multiple_of(kj * key_tile, key_tile), key_tile)
            k_tile, v_tile = k_s[keys, :], v_s[keys, :]
            bias = tile_bias(key_pos_ref, keys, query_pos)
            out = []
            add_k, add_v = gk_s[keys, :], gv_s[keys, :]
            for h in range(2):
                scores = dot(k_tile, q_parts[h], ((1,), (1,))) + slope_ref[h] * bias
                weights = jnp.exp(scores - log_ref[h : h + 1, queries])
                grads = dot(v_tile, g_parts[h], ((1,), (1,)))
                raw = (weights * (grads - deltas[h])).astype(BF16)
                add_v = add_v + dot(weights.astype(BF16), g_parts[h], ((1,), (0,)))
                add_k = add_k + dot(raw, q_parts[h], ((1,), (0,)))
                out.append(carry[h] + dot(kt_s[h * half : (h + 1) * half, keys], raw, ((1,), (0,))))
            gk_s[keys, :] = add_k
            gv_s[keys, :] = add_v
            return tuple(out)

        start = jnp.zeros((half, query_tile), F32)
        ends = lax.fori_loop(0, count_ref[qi], key_step, (start, start))
        grad_q = jnp.concatenate(ends, axis=0) * 0.125
        q_s[queries, :] = grad_q.T.astype(BF16)
        return 0

    lax.fori_loop(0, q_s.shape[0] // query_tile, query_step, 0)
    first_key = 2 * query_block
    first_value = first_key + 2 * half_tok

    def put(step, _):
        src, rows = slot_rows(order_ref, step, query_block, 0)
        at = pl.ds(pl.multiple_of(step * query_block, 16), query_block)
        out_ref[src, rows, :] = q_s[at, :]
        at = pl.ds(pl.multiple_of(step * half_tok, 16), half_tok)
        src, rows = slot_rows(order_ref, step, half_tok, first_key)
        out_ref[src, rows, :] = gk_s[at, :].astype(BF16)
        src, rows = slot_rows(order_ref, step, half_tok, first_value)
        out_ref[src, rows, :] = gv_s[at, :].astype(BF16)
        return 0

    lax.fori_loop(0, order_ref.shape[0], put, 0)


def call_local(kernel, outs, scratch, flops, *args):
    smem = pl.BlockSpec(memory_space=pltpu.SMEM)
    vmem = pl.BlockSpec(memory_space=pltpu.VMEM)
    return pl.pallas_call(
        kernel,
        out_shape=outs,
        in_specs=[smem] * 3 + [vmem] * (len(args) - 3),
        out_specs=[vmem] * len(outs),
        scratch_shapes=scratch,
        cost_estimate=pl.CostEstimate(flops=flops, bytes_accessed=6_000_000, transcendentals=flops // 256),
        compiler_params=pltpu.CompilerParams(vmem_limit_bytes=48 * 1024 * 1024),
    )(*args)


def body(
    tokens, block_map, positions, norm_gain_one, norm_shift_one, qkv_weight, query_bias,
    value_bias, dense_weight, dense_bias, norm_gain_two, norm_shift_two, up_weight, up_bias,
    down_weight, down_bias, cotangent,
):
    width = tokens.shape[2]
    count_tok = tokens.shape[1]
    half_tok = count_tok // 2
    ctx = lax.axis_size("ctx")
    wsh = lax.axis_size("wsh")
    blocks = 2 * ctx
    length = ctx * count_tok
    own = width // wsh
    pairs = own // LANES
    units = wsh * pairs
    share = max(1, ctx // units)
    query_block = half_tok // share
    query_count = length // share
    query_tile = min(QUERY_TILE, query_count)
    key_tile = min(KEY_TILE, length)
    all_tok = wsh * count_tok

    def gather(value):
        return lax.all_gather(value, "wsh", axis=0, tiled=True)

    def scatter(value):
        return lax.psum_scatter(value, "wsh", scatter_dimension=0, tiled=True)

    def swap_ctx(value):
        return lax.all_to_all(value, "ctx", split_axis=0, concat_axis=0, tiled=True)

    vectors = jnp.stack(
        [norm_gain_one, norm_shift_one, dense_bias, norm_gain_two, norm_shift_two, down_bias]
    )
    vectors = lax.all_gather(vectors, "wsh", axis=1, tiled=True).astype(F32)
    gain_first, shift_first, dense_shift, gain_second, shift_second, down_shift = vectors
    all_pos = gather(positions)
    qkv_own = lax.all_to_all(
        qkv_weight.reshape(own, 3, wsh, own), "wsh", split_axis=2, concat_axis=0, tiled=True
    ).reshape(width, 3 * own)
    hidden_own = up_weight.shape[1] // wsh
    up_own = lax.all_to_all(
        up_weight.reshape(own, wsh, hidden_own), "wsh", split_axis=1, concat_axis=0, tiled=True
    ).reshape(width, hidden_own)

    unit = lax.axis_index("ctx") // share
    part = lax.axis_index("ctx") % share
    seq_pos = lax.dynamic_index_in_dim(all_pos, unit // pairs, 0, keepdims=False)
    stored = block_map.reshape(-1)
    ids = jnp.arange(blocks, dtype=jnp.int32)
    order = jnp.sum(jnp.where(stored[None, :] == ids[:, None], ids[None, :], 0), axis=1)
    query_pos = lax.dynamic_index_in_dim(
        seq_pos.reshape(blocks, share, query_block), part, 1, keepdims=False
    ).reshape(query_count)
    last_pos = query_pos.reshape(-1, query_tile)[:, -1]
    first_pos = seq_pos.reshape(-1, key_tile)[:, 0]
    counts = jnp.sum((first_pos[None, :] <= last_pos[:, None]).astype(jnp.int32), axis=1)
    head_ids = lax.axis_index("wsh") * (HEADS // wsh) + (unit % pairs) * 2 + jnp.arange(2)
    slopes = 2.0 ** (-8.0 * (head_ids.astype(F32) + 1.0) / HEADS)
    query_row = query_pos.astype(F32).reshape(1, query_count)
    key_column = seq_pos.astype(F32).reshape(length, 1)

    def to_query_units(value):
        shaped = value.reshape(wsh, 2, share, query_block, pairs, LANES)
        return shaped.transpose(0, 4, 2, 1, 3, 5).reshape(ctx, 2 * query_block, LANES)

    def from_query_units(value):
        shaped = value.reshape(wsh, pairs, share, 2, query_block, LANES)
        return shaped.transpose(0, 3, 2, 4, 1, 5).reshape(all_tok, own)

    def to_key_units(value):
        shaped = value.reshape(wsh, count_tok, pairs, LANES).transpose(0, 2, 1, 3)
        shaped = jnp.broadcast_to(shaped[:, :, None], (wsh, pairs, share, count_tok, LANES))
        return shaped.reshape(ctx, count_tok, LANES)

    def from_key_units(value):
        shaped = value.reshape(wsh, pairs, share, count_tok, LANES)
        if share == 1:
            shaped = shaped[:, :, 0]
        else:
            shaped = jnp.sum(shaped.astype(F32), axis=2).astype(BF16)
        return shaped.transpose(0, 2, 1, 3).reshape(all_tok, own)

    inputs = tokens[0].astype(F32)
    normed, scaled_first, inverse_first = norm_forward(inputs, gain_first, shift_first)
    normed_all = gather(normed.astype(BF16))
    grad_all = gather(cotangent[0])
    mixed = jnp.dot(normed_all, qkv_own, preferred_element_type=F32)
    query = (mixed[:, :own] + query_bias.astype(F32)).astype(BF16)
    keys = mixed[:, own : 2 * own].astype(BF16)
    values = (mixed[:, 2 * own :] + value_bias.astype(F32)).astype(BF16)
    packed = swap_ctx(
        jnp.concatenate([to_query_units(query), to_key_units(keys), to_key_units(values)], axis=1)
    )
    sizes = (query_block, half_tok, query_tile, key_tile)
    flops = 4 * query_count * length * LANES
    context_units, attended, logs = call_local(
        functools.partial(forward_kernel, *sizes),
        [
            jax.ShapeDtypeStruct((ctx, 2 * query_block, LANES), BF16),
            jax.ShapeDtypeStruct((LANES, query_count), F32),
            jax.ShapeDtypeStruct((2, query_count), F32),
        ],
        [
            pltpu.VMEM((query_count, LANES), BF16),
            pltpu.VMEM((length, LANES), BF16),
            pltpu.VMEM((length, LANES), BF16),
            pltpu.VMEM((LANES, length), BF16),
        ],
        flops,
        order, counts, slopes, packed, query_row, key_column,
    )
    context = from_query_units(swap_ctx(context_units))
    projected = scatter(jnp.dot(context, dense_weight, preferred_element_type=F32).astype(BF16))
    middle = inputs + projected.astype(F32) + dense_shift
    normed_two, scaled_second, inverse_second = norm_forward(middle, gain_second, shift_second)
    normed_two_all = gather(normed_two.astype(BF16))
    hidden = jnp.dot(normed_two_all, up_own, preferred_element_type=F32) + up_bias.astype(F32)
    activated, gelu_back = jax.vjp(gelu_tanh, hidden)
    active = activated.astype(BF16)
    branch = scatter(jnp.dot(active, down_weight, preferred_element_type=F32).astype(BF16))
    layer_out = (middle + branch.astype(F32) + down_shift).astype(BF16)[None]

    grad_active = dot(grad_all, down_weight, ((1,), (1,)))
    grad_hidden = gelu_back(grad_active)[0].astype(BF16)
    grad_normed_two = scatter(dot(grad_hidden, up_own, ((1,), (1,))).astype(BF16)).astype(F32)
    grad_middle_part, grad_gain_second, grad_shift_second = norm_backward(
        grad_normed_two, scaled_second, inverse_second, gain_second
    )
    grad_middle = cotangent[0].astype(F32) + grad_middle_part
    grad_proj_all = gather(grad_middle.astype(BF16))
    grad_context = dot(grad_proj_all, dense_weight, ((1,), (1,))).astype(BF16)
    grad_units = swap_ctx(to_query_units(grad_context))
    (grad_packed,) = call_local(
        functools.partial(backward_kernel, *sizes),
        [jax.ShapeDtypeStruct(packed.shape, BF16)],
        [
            pltpu.VMEM((query_count, LANES), BF16),
            pltpu.VMEM((length, LANES), BF16),
            pltpu.VMEM((length, LANES), BF16),
            pltpu.VMEM((LANES, length), BF16),
            pltpu.VMEM((query_count, LANES), BF16),
            pltpu.VMEM((length, LANES), F32),
            pltpu.VMEM((length, LANES), F32),
        ],
        flops * 5 // 2,
        order, counts, slopes, packed, query_row, key_column, attended, logs, grad_units,
    )
    grad_packed = swap_ctx(grad_packed)
    first_key = 2 * query_block
    first_value = first_key + count_tok
    grad_query = from_query_units(grad_packed[:, :first_key])
    grad_keys = from_key_units(grad_packed[:, first_key:first_value])
    grad_values = from_key_units(grad_packed[:, first_value:])
    grad_mixed = jnp.concatenate([grad_query, grad_keys, grad_values], axis=1)
    grad_normed = scatter(dot(grad_mixed, qkv_own, ((1,), (1,))).astype(BF16)).astype(F32)
    grad_input_part, grad_gain_first, grad_shift_first = norm_backward(
        grad_normed, scaled_first, inverse_first, gain_first
    )
    input_grad = (grad_middle + grad_input_part).astype(BF16)[None]

    def sum_rows(value):
        part = lax.psum_scatter(value.astype(BF16), "ctx", scatter_dimension=0, tiled=True)
        return lax.all_gather(part, "ctx", axis=0, tiled=True).astype(F32)

    def sum_turned(value, groups):
        rows = own // ctx
        part = lax.psum_scatter(
            value.astype(BF16).reshape(wsh, ctx, rows, value.shape[1]),
            "ctx", scatter_dimension=1, tiled=True,
        ).reshape(wsh, rows, value.shape[1])
        part = lax.all_to_all(part, "wsh", split_axis=0, concat_axis=0, tiled=True)
        part = lax.all_gather(part, "ctx", axis=0, tiled=False)
        each = value.shape[1] // groups
        full = part.astype(F32).reshape(ctx, wsh, rows, groups, each)
        return full.transpose(0, 2, 3, 1, 4).reshape(own, wsh * value.shape[1])

    grad_down_weight = sum_rows(dot(active, grad_all, ((0,), (0,))))
    grad_up_weight = sum_turned(dot(normed_two_all, grad_hidden, ((0,), (0,))), 1)
    grad_dense_weight = sum_rows(dot(context, grad_proj_all, ((0,), (0,))))
    grad_qkv_weight = sum_turned(dot(normed_all, grad_mixed, ((0,), (0,))), 3)
    norms = jnp.stack([grad_gain_first, grad_shift_first, grad_gain_second, grad_shift_second])
    norms = lax.psum_scatter(norms, "wsh", scatter_dimension=1, tiled=True)
    start = lax.axis_index("wsh") * own
    vectors_own = jnp.concatenate(
        [
            norms.reshape(-1),
            column_sum(grad_query),
            column_sum(grad_values),
            column_sum(lax.dynamic_slice_in_dim(grad_proj_all, start, own, 1)),
            column_sum(lax.dynamic_slice_in_dim(grad_all, start, own, 1)),
            column_sum(grad_hidden),
        ]
    )
    sums = lax.psum(vectors_own, "ctx")
    (
        sum_gain_first, sum_shift_first, sum_gain_second, sum_shift_second,
        sum_query, sum_value, sum_dense, sum_down,
    ) = sums[: 8 * own].reshape(8, own)
    return (
        layer_out, input_grad, sum_gain_first, sum_shift_first, grad_qkv_weight, sum_query,
        sum_value, grad_dense_weight, sum_dense, sum_gain_second, sum_shift_second,
        grad_up_weight, sums[8 * own :], grad_down_weight, sum_down,
    )


def solution(mesh):
    rows, vec, tok = P("wsh", None), P("wsh"), P("wsh", "ctx", None)
    in_specs = (
        tok, P(), rows, vec, vec, rows, vec, vec, rows, vec, vec, vec, rows, vec, rows, vec, tok,
    )
    out_specs = (
        tok, tok, vec, vec, rows, vec, vec, rows, vec, vec, vec, rows, vec, rows, vec,
    )
    return jax.shard_map(body, mesh=mesh, in_specs=in_specs, out_specs=out_specs, check_vma=False)
```

```python
import functools

import jax
import jax.numpy as jnp
from jax import lax
from jax.experimental import pallas as pl
from jax.experimental.pallas import tpu as pltpu
from jax.sharding import PartitionSpec as P

HEADS = 16
EPS = 1e-05
LANES = 128
QUERY_TILE = 256
KEY_TILE = 512
FAR = -1e30
F32 = jnp.float32
BF16 = jnp.bfloat16


def norm_forward(values, gain_vec, shift_vec):
    row_mean = jnp.mean(values, axis=-1, keepdims=True)
    centered = values - row_mean
    variance = jnp.mean(centered * centered, axis=-1, keepdims=True)
    inverse = lax.rsqrt(variance + EPS)
    scaled = centered * inverse
    return (scaled * gain_vec + shift_vec, scaled, inverse)


def norm_backward(grad_out, scaled, inverse, gain_vec):
    grad_scaled = grad_out * gain_vec
    mean_grad = jnp.mean(grad_scaled, axis=-1, keepdims=True)
    mean_along = jnp.mean(grad_scaled * scaled, axis=-1, keepdims=True)
    grad_in = inverse * (grad_scaled - mean_grad - scaled * mean_along)
    return (grad_in, jnp.sum(grad_out * scaled, axis=0), jnp.sum(grad_out, axis=0))


def gelu_tanh(values):
    return jax.nn.gelu(values, approximate=True)


def dot(a, b, dims):
    return lax.dot_general(a, b, (dims, ((), ())), preferred_element_type=F32)


def column_sum(values):
    return jnp.sum(values.astype(F32), axis=0)


def slot_rows(order_ref, step, rows, first):
    slot = order_ref[step]
    src = slot // 2
    return src, pl.ds(pl.multiple_of(first + (slot % 2) * rows, 16), rows)


def split_heads(tile):
    lane = lax.broadcasted_iota(jnp.int32, tile.shape, 1)
    zero = jnp.zeros_like(tile)
    half = LANES // 2
    return (jnp.where(lane < half, tile, zero), jnp.where(lane >= half, tile, zero))


def load_sequence(query_block, half_tok, order_ref, packed_ref, q_s, k_s, v_s):
    first_key = 2 * query_block
    first_value = first_key + 2 * half_tok

    def load(step, _):
        src, rows = slot_rows(order_ref, step, query_block, 0)
        to = pl.ds(pl.multiple_of(step * query_block, 16), query_block)
        q_s[to, :] = packed_ref[src, rows, :]
        to = pl.ds(pl.multiple_of(step * half_tok, 16), half_tok)
        src, rows = slot_rows(order_ref, step, half_tok, first_key)
        k_s[to, :] = packed_ref[src, rows, :]
        src, rows = slot_rows(order_ref, step, half_tok, first_value)
        v_s[to, :] = packed_ref[src, rows, :]
        return 0

    lax.fori_loop(0, order_ref.shape[0], load, 0)


def transpose_into(to_ref, from_ref, key_tile):
    def turn(step, _):
        rows = pl.ds(pl.multiple_of(step * key_tile, key_tile), key_tile)
        to_ref[:, rows] = from_ref[rows, :].astype(F32).T.astype(BF16)
        return 0

    lax.fori_loop(0, from_ref.shape[0] // key_tile, turn, 0)


def tile_bias(key_pos_ref, keys, query_pos):
    distance = key_pos_ref[keys, :] - query_pos
    return jnp.where(distance <= 0.0, distance, FAR)


def forward_kernel(
    query_block, half_tok, query_tile, key_tile,
    order_ref, count_ref, slope_ref, packed_ref, query_pos_ref, key_pos_ref,
    context_ref, attended_ref, log_ref, q_s, k_s, v_s, vt_s,
):
    load_sequence(query_block, half_tok, order_ref, packed_ref, q_s, k_s, v_s)
    transpose_into(vt_s, v_s, key_tile)
    half = LANES // 2

    def query_step(qi, _):
        queries = pl.ds(pl.multiple_of(qi * query_tile, query_tile), query_tile)
        q_parts = split_heads(q_s[queries, :] * 0.125)
        query_pos = query_pos_ref[:, queries]

        def key_step(kj, carry):
            keys = pl.ds(pl.multiple_of(kj * key_tile, key_tile), key_tile)
            k_tile = k_s[keys, :]
            bias = tile_bias(key_pos_ref, keys, query_pos)
            out = []
            for h in range(2):
                top, total, acc = carry[h]
                scores = dot(k_tile, q_parts[h], ((1,), (1,))) + slope_ref[h] * bias
                new_top = jnp.maximum(top, jnp.max(scores, axis=0, keepdims=True))
                rescale = jnp.exp(top - new_top)
                weights = jnp.exp(scores - new_top)
                total = total * rescale + jnp.sum(weights, axis=0, keepdims=True)
                v_tile = vt_s[h * half : (h + 1) * half, keys]
                acc = acc * rescale + dot(v_tile, weights.astype(BF16), ((1,), (0,)))
                out.append((new_top, total, acc))
            return tuple(out)

        row = jnp.zeros((1, query_tile), F32)
        start = (row + FAR, row, jnp.zeros((half, query_tile), F32))
        ends = lax.fori_loop(0, count_ref[qi], key_step, (start, start))
        for h in range(2):
            top, total, acc = ends[h]
            attended_ref[h * half : (h + 1) * half, queries] = acc / total
            log_ref[h : h + 1, queries] = top + jnp.log(total)
        q_s[queries, :] = attended_ref[:, queries].T.astype(BF16)
        return 0

    lax.fori_loop(0, q_s.shape[0] // query_tile, query_step, 0)

    def put(step, _):
        src, rows = slot_rows(order_ref, step, query_block, 0)
        at = pl.ds(pl.multiple_of(step * query_block, 16), query_block)
        context_ref[src, rows, :] = q_s[at, :]
        return 0

    lax.fori_loop(0, order_ref.shape[0], put, 0)


def backward_kernel(
    query_block, half_tok, query_tile, key_tile,
    order_ref, count_ref, slope_ref, packed_ref, query_pos_ref, key_pos_ref,
    attended_ref, log_ref, grad_ref,
    out_ref, q_s, k_s, v_s, kt_s, g_s, gk_s, gv_s,
):
    load_sequence(query_block, half_tok, order_ref, packed_ref, q_s, k_s, v_s)
    transpose_into(kt_s, k_s, key_tile)
    half = LANES // 2

    def load(step, _):
        src, rows = slot_rows(order_ref, step, query_block, 0)
        at = pl.ds(pl.multiple_of(step * query_block, 16), query_block)
        g_s[at, :] = grad_ref[src, rows, :]
        return 0

    lax.fori_loop(0, order_ref.shape[0], load, 0)
    gk_s[...] = jnp.zeros_like(gk_s)
    gv_s[...] = jnp.zeros_like(gv_s)

    def query_step(qi, _):
        queries = pl.ds(pl.multiple_of(qi * query_tile, query_tile), query_tile)
        q_parts = split_heads(q_s[queries, :] * 0.125)
        g_tile = g_s[queries, :]
        g_parts = split_heads(g_tile)
        along = g_tile.astype(F32).T * attended_ref[:, queries]
        deltas = [
            jnp.sum(along[h * half : (h + 1) * half], axis=0, keepdims=True) for h in range(2)
        ]
        query_pos = query_pos_ref[:, queries]

        def key_step(kj, carry):
            keys = pl.ds(pl.multiple_of(kj * key_tile, key_tile), key_tile)
            k_tile, v_tile = k_s[keys, :], v_s[keys, :]
            bias = tile_bias(key_pos_ref, keys, query_pos)
            out = []
            add_k, add_v = gk_s[keys, :], gv_s[keys, :]
            for h in range(2):
                scores = dot(k_tile, q_parts[h], ((1,), (1,))) + slope_ref[h] * bias
                weights = jnp.exp(scores - log_ref[h : h + 1, queries])
                grads = dot(v_tile, g_parts[h], ((1,), (1,)))
                raw = (weights * (grads - deltas[h])).astype(BF16)
                add_v = add_v + dot(weights.astype(BF16), g_parts[h], ((1,), (0,)))
                add_k = add_k + dot(raw, q_parts[h], ((1,), (0,)))
                out.append(carry[h] + dot(kt_s[h * half : (h + 1) * half, keys], raw, ((1,), (0,))))
            gk_s[keys, :] = add_k
            gv_s[keys, :] = add_v
            return tuple(out)

        start = jnp.zeros((half, query_tile), F32)
        ends = lax.fori_loop(0, count_ref[qi], key_step, (start, start))
        grad_q = jnp.concatenate(ends, axis=0) * 0.125
        q_s[queries, :] = grad_q.T.astype(BF16)
        return 0

    lax.fori_loop(0, q_s.shape[0] // query_tile, query_step, 0)
    first_key = 2 * query_block
    first_value = first_key + 2 * half_tok

    def put(step, _):
        src, rows = slot_rows(order_ref, step, query_block, 0)
        at = pl.ds(pl.multiple_of(step * query_block, 16), query_block)
        out_ref[src, rows, :] = q_s[at, :]
        at = pl.ds(pl.multiple_of(step * half_tok, 16), half_tok)
        src, rows = slot_rows(order_ref, step, half_tok, first_key)
        out_ref[src, rows, :] = gk_s[at, :].astype(BF16)
        src, rows = slot_rows(order_ref, step, half_tok, first_value)
        out_ref[src, rows, :] = gv_s[at, :].astype(BF16)
        return 0

    lax.fori_loop(0, order_ref.shape[0], put, 0)


def call_local(kernel, outs, scratch, flops, *args):
    smem = pl.BlockSpec(memory_space=pltpu.SMEM)
    vmem = pl.BlockSpec(memory_space=pltpu.VMEM)
    return pl.pallas_call(
        kernel,
        out_shape=outs,
        in_specs=[smem] * 3 + [vmem] * (len(args) - 3),
        out_specs=[vmem] * len(outs),
        scratch_shapes=scratch,
        cost_estimate=pl.CostEstimate(flops=flops, bytes_accessed=6_000_000, transcendentals=flops // 256),
        compiler_params=pltpu.CompilerParams(vmem_limit_bytes=48 * 1024 * 1024),
    )(*args)


def add_low(a, b):
    return (a.astype(F32) + b.astype(F32)).astype(BF16)


def ring_place(index, count):
    odd = index % 2
    return (1 - odd) * (index // 2) + odd * (count - 1 - index // 2)


def ring_index(place, count):
    late = place // (count // 2)
    return (1 - late) * 2 * place + late * (2 * (count - 1 - place) + 1)


def sum_kernel(
    count, peers, turned, part_ref, out_ref, held, mine,
    send_sem, recv_sem, turn_send, turn_recv, back_send, back_recv,
):
    place = ring_place(lax.axis_index("ctx"), count)
    me = lax.axis_index("wsh")
    sides = (
        ring_index((place + 1) % count, count), ring_index((place + count - 1) % count, count)
    )
    barrier = pltpu.get_barrier_semaphore()
    for side in sides:
        pl.semaphore_signal(
            barrier, inc=1, device_id={"ctx": side}, device_id_type=pl.DeviceIdType.MESH
        )
    for step in range(1, peers):
        pl.semaphore_signal(
            barrier, inc=1, device_id={"wsh": (me + step) % peers},
            device_id_type=pl.DeviceIdType.MESH,
        )
    pl.semaphore_wait(barrier, 1 + peers)

    def chunk(way, back):
        return (place + count - back) % count if way == 0 else (place + back) % count

    def send(way, step, src):
        return pltpu.make_async_remote_copy(
            src_ref=src, dst_ref=held.at[step, way],
            send_sem=send_sem.at[step, way], recv_sem=recv_sem.at[step, way],
            device_id={"ctx": sides[way]}, device_id_type=pl.DeviceIdType.MESH,
        )

    for way in range(2):
        send(way, 0, part_ref.at[chunk(way, 1), way]).start()

    def reduce_step(step, _):
        for way in range(2):
            here = held.at[step - 1, way]
            send(way, step - 1, here).wait_recv()
            here[...] = add_low(here[...], part_ref[chunk(way, step + 1), way])
            send(way, step, here).start()
        return 0

    lax.fori_loop(1, count - 1, reduce_step, 0)
    for way in range(2):
        last = held.at[count - 2, way]
        send(way, count - 2, last).wait_recv()
        mine[way] = add_low(last[...], part_ref[place, way])

    def turn(step):
        peer = (me + step) % peers
        return pltpu.make_async_remote_copy(
            src_ref=mine.at[:, pl.ds(pl.multiple_of(peer * turned, 16), turned), :],
            dst_ref=out_ref.at[place, :, pl.ds(pl.multiple_of(me * turned, 16), turned), :],
            send_sem=turn_send.at[step - 1], recv_sem=turn_recv.at[step - 1],
            device_id={"wsh": peer}, device_id_type=pl.DeviceIdType.MESH,
        )

    for step in range(1, peers):
        turn(step).start()
    kept = pl.ds(pl.multiple_of(me * turned, 16), turned)
    out_ref[place, :, kept, :] = mine[:, kept, :]
    out_ref[place, :, peers * turned :, :] = mine[:, peers * turned :, :]
    for step in range(1, peers):
        turn(step).wait_recv()

    def pass_on(way, step):
        here = out_ref.at[chunk(way, step), way]
        return pltpu.make_async_remote_copy(
            src_ref=here, dst_ref=here,
            send_sem=back_send.at[step, way], recv_sem=back_recv.at[step, way],
            device_id={"ctx": sides[way]}, device_id_type=pl.DeviceIdType.MESH,
        )

    for way in range(2):
        pass_on(way, 0).start()

    def gather_step(step, _):
        for way in range(2):
            pass_on(way, step - 1).wait_recv()
            pass_on(way, step).start()
        return 0

    lax.fori_loop(1, count - 1, gather_step, 0)
    for way in range(2):
        pass_on(way, count - 2).wait_recv()
    for step in range(1, peers):
        turn(step).wait_send()

    def drain(step, _):
        for way in range(2):
            send(way, step, held.at[step, way]).wait_send()
            pass_on(way, step).wait_send()
        return 0

    lax.fori_loop(0, count - 1, drain, 0)


def sum_over_ctx(parts, turned):
    count, _, rows, width = parts.shape
    peers = lax.axis_size("wsh")
    sems = pltpu.SemaphoreType.DMA((count - 1, 2))
    turn_sems = pltpu.SemaphoreType.DMA((peers - 1,))
    return pl.pallas_call(
        functools.partial(sum_kernel, count, peers, turned),
        out_shape=jax.ShapeDtypeStruct(parts.shape, BF16),
        in_specs=[pl.BlockSpec(memory_space=pltpu.VMEM)],
        out_specs=pl.BlockSpec(memory_space=pltpu.VMEM),
        scratch_shapes=[
            pltpu.VMEM((count - 1, 2, rows, width), BF16),
            pltpu.VMEM((2, rows, width), BF16),
            sems, sems, turn_sems, turn_sems, sems, sems,
        ],
        cost_estimate=pl.CostEstimate(flops=parts.size, bytes_accessed=300_000_000, transcendentals=0),
        compiler_params=pltpu.CompilerParams(
            collective_id=0, has_side_effects=True, vmem_limit_bytes=40 * 1024 * 1024
        ),
    )(parts)


def body(
    tokens, block_map, positions, norm_gain_one, norm_shift_one, qkv_weight, query_bias,
    value_bias, dense_weight, dense_bias, norm_gain_two, norm_shift_two, up_weight, up_bias,
    down_weight, down_bias, cotangent,
):
    width = tokens.shape[2]
    count_tok = tokens.shape[1]
    half_tok = count_tok // 2
    ctx = lax.axis_size("ctx")
    wsh = lax.axis_size("wsh")
    blocks = 2 * ctx
    length = ctx * count_tok
    own = width // wsh
    pairs = own // LANES
    units = wsh * pairs
    share = max(1, ctx // units)
    query_block = half_tok // share
    query_count = length // share
    query_tile = min(QUERY_TILE, query_count)
    key_tile = min(KEY_TILE, length)
    all_tok = wsh * count_tok

    def gather(value):
        return lax.all_gather(value, "wsh", axis=0, tiled=True)

    def scatter(value):
        return lax.psum_scatter(value, "wsh", scatter_dimension=0, tiled=True)

    def swap_ctx(value):
        return lax.all_to_all(value, "ctx", split_axis=0, concat_axis=0, tiled=True)

    vectors = jnp.stack(
        [norm_gain_one, norm_shift_one, dense_bias, norm_gain_two, norm_shift_two, down_bias]
    )
    vectors = lax.all_gather(vectors, "wsh", axis=1, tiled=True).astype(F32)
    gain_first, shift_first, dense_shift, gain_second, shift_second, down_shift = vectors
    all_pos = gather(positions)
    qkv_own = lax.all_to_all(
        qkv_weight.reshape(own, 3, wsh, own), "wsh", split_axis=2, concat_axis=0, tiled=True
    ).reshape(width, 3 * own)
    hidden_own = up_weight.shape[1] // wsh
    up_own = lax.all_to_all(
        up_weight.reshape(own, wsh, hidden_own), "wsh", split_axis=1, concat_axis=0, tiled=True
    ).reshape(width, hidden_own)

    unit = lax.axis_index("ctx") // share
    part = lax.axis_index("ctx") % share
    seq_pos = lax.dynamic_index_in_dim(all_pos, unit // pairs, 0, keepdims=False)
    stored = block_map.reshape(-1)
    ids = jnp.arange(blocks, dtype=jnp.int32)
    order = jnp.sum(jnp.where(stored[None, :] == ids[:, None], ids[None, :], 0), axis=1)
    query_pos = lax.dynamic_index_in_dim(
        seq_pos.reshape(blocks, share, query_block), part, 1, keepdims=False
    ).reshape(query_count)
    last_pos = query_pos.reshape(-1, query_tile)[:, -1]
    first_pos = seq_pos.reshape(-1, key_tile)[:, 0]
    counts = jnp.sum((first_pos[None, :] <= last_pos[:, None]).astype(jnp.int32), axis=1)
    head_ids = lax.axis_index("wsh") * (HEADS // wsh) + (unit % pairs) * 2 + jnp.arange(2)
    slopes = 2.0 ** (-8.0 * (head_ids.astype(F32) + 1.0) / HEADS)
    query_row = query_pos.astype(F32).reshape(1, query_count)
    key_column = seq_pos.astype(F32).reshape(length, 1)

    def to_query_units(value):
        shaped = value.reshape(wsh, 2, share, query_block, pairs, LANES)
        return shaped.transpose(0, 4, 2, 1, 3, 5).reshape(ctx, 2 * query_block, LANES)

    def from_query_units(value):
        shaped = value.reshape(wsh, pairs, share, 2, query_block, LANES)
        return shaped.transpose(0, 3, 2, 4, 1, 5).reshape(all_tok, own)

    def to_key_units(value):
        shaped = value.reshape(wsh, count_tok, pairs, LANES).transpose(0, 2, 1, 3)
        shaped = jnp.broadcast_to(shaped[:, :, None], (wsh, pairs, share, count_tok, LANES))
        return shaped.reshape(ctx, count_tok, LANES)

    def from_key_units(value):
        shaped = value.reshape(wsh, pairs, share, count_tok, LANES)
        if share == 1:
            shaped = shaped[:, :, 0]
        else:
            shaped = jnp.sum(shaped.astype(F32), axis=2).astype(BF16)
        return shaped.transpose(0, 2, 1, 3).reshape(all_tok, own)

    inputs = tokens[0].astype(F32)
    normed, scaled_first, inverse_first = norm_forward(inputs, gain_first, shift_first)
    normed_all = gather(normed.astype(BF16))
    grad_all = gather(cotangent[0])
    mixed = jnp.dot(normed_all, qkv_own, preferred_element_type=F32)
    query = (mixed[:, :own] + query_bias.astype(F32)).astype(BF16)
    keys = mixed[:, own : 2 * own].astype(BF16)
    values = (mixed[:, 2 * own :] + value_bias.astype(F32)).astype(BF16)
    packed = swap_ctx(
        jnp.concatenate([to_query_units(query), to_key_units(keys), to_key_units(values)], axis=1)
    )
    sizes = (query_block, half_tok, query_tile, key_tile)
    flops = 4 * query_count * length * LANES
    context_units, attended, logs = call_local(
        functools.partial(forward_kernel, *sizes),
        [
            jax.ShapeDtypeStruct((ctx, 2 * query_block, LANES), BF16),
            jax.ShapeDtypeStruct((LANES, query_count), F32),
            jax.ShapeDtypeStruct((2, query_count), F32),
        ],
        [
            pltpu.VMEM((query_count, LANES), BF16),
            pltpu.VMEM((length, LANES), BF16),
            pltpu.VMEM((length, LANES), BF16),
            pltpu.VMEM((LANES, length), BF16),
        ],
        flops,
        order, counts, slopes, packed, query_row, key_column,
    )
    context = from_query_units(swap_ctx(context_units))
    projected = scatter(jnp.dot(context, dense_weight, preferred_element_type=F32).astype(BF16))
    middle = inputs + projected.astype(F32) + dense_shift
    normed_two, scaled_second, inverse_second = norm_forward(middle, gain_second, shift_second)
    normed_two_all = gather(normed_two.astype(BF16))
    hidden = jnp.dot(normed_two_all, up_own, preferred_element_type=F32) + up_bias.astype(F32)
    activated, gelu_back = jax.vjp(gelu_tanh, hidden)
    active = activated.astype(BF16)
    branch = scatter(jnp.dot(active, down_weight, preferred_element_type=F32).astype(BF16))
    layer_out = (middle + branch.astype(F32) + down_shift).astype(BF16)[None]

    grad_active = dot(grad_all, down_weight, ((1,), (1,)))
    grad_hidden = gelu_back(grad_active)[0].astype(BF16)
    grad_normed_two = scatter(dot(grad_hidden, up_own, ((1,), (1,))).astype(BF16)).astype(F32)
    grad_middle_part, grad_gain_second, grad_shift_second = norm_backward(
        grad_normed_two, scaled_second, inverse_second, gain_second
    )
    grad_middle = cotangent[0].astype(F32) + grad_middle_part
    grad_proj_all = gather(grad_middle.astype(BF16))
    grad_context = dot(grad_proj_all, dense_weight, ((1,), (1,))).astype(BF16)
    grad_units = swap_ctx(to_query_units(grad_context))
    (grad_packed,) = call_local(
        functools.partial(backward_kernel, *sizes),
        [jax.ShapeDtypeStruct(packed.shape, BF16)],
        [
            pltpu.VMEM((query_count, LANES), BF16),
            pltpu.VMEM((length, LANES), BF16),
            pltpu.VMEM((length, LANES), BF16),
            pltpu.VMEM((LANES, length), BF16),
            pltpu.VMEM((query_count, LANES), BF16),
            pltpu.VMEM((length, LANES), F32),
            pltpu.VMEM((length, LANES), F32),
        ],
        flops * 5 // 2,
        order, counts, slopes, packed, query_row, key_column, attended, logs, grad_units,
    )
    grad_packed = swap_ctx(grad_packed)
    first_key = 2 * query_block
    first_value = first_key + count_tok
    grad_query = from_query_units(grad_packed[:, :first_key])
    grad_keys = from_key_units(grad_packed[:, first_key:first_value])
    grad_values = from_key_units(grad_packed[:, first_value:])
    grad_mixed = jnp.concatenate([grad_query, grad_keys, grad_values], axis=1)
    grad_normed = scatter(dot(grad_mixed, qkv_own, ((1,), (1,))).astype(BF16)).astype(F32)
    grad_input_part, grad_gain_first, grad_shift_first = norm_backward(
        grad_normed, scaled_first, inverse_first, gain_first
    )
    input_grad = (grad_middle + grad_input_part).astype(BF16)[None]

    chunk = 2 * LANES

    def cut(value):
        shaped = value.astype(BF16).reshape(ctx, 2, -1, value.shape[1] // chunk, chunk)
        return shaped.transpose(0, 1, 3, 2, 4).reshape(ctx, 2, -1, chunk)

    def uncut(value, columns):
        shaped = value.astype(F32).reshape(ctx, 2, columns // chunk, -1, chunk)
        return shaped.transpose(0, 1, 3, 2, 4).reshape(-1, columns)

    def pad_rows(value):
        return jnp.pad(value, [(0, 0)] * (value.ndim - 2) + [(0, -value.shape[-2] % 16), (0, 0)])

    turned_cols = hidden_own + 3 * own
    groups = turned_cols // chunk
    fine = own // (2 * ctx)
    turned = jnp.concatenate(
        [
            dot(normed_two_all, grad_hidden, ((0,), (0,))).astype(BF16),
            dot(normed_all, grad_mixed, ((0,), (0,))).astype(BF16),
        ],
        axis=1,
    ).reshape(wsh, ctx, 2, fine, groups, chunk)
    turned = pad_rows(
        turned.transpose(1, 2, 0, 4, 3, 5).reshape(ctx, 2, wsh, groups * fine, chunk)
    )
    turned_rows = turned.shape[3]
    down_part = cut(dot(active, grad_all, ((0,), (0,))))
    dense_part = cut(dot(context, grad_proj_all, ((0,), (0,))))
    norms = jnp.stack([grad_gain_first, grad_shift_first, grad_gain_second, grad_shift_second])
    norms = lax.psum_scatter(norms, "wsh", scatter_dimension=1, tiled=True)
    start = lax.axis_index("wsh") * own
    vectors_own = jnp.concatenate(
        [
            norms.reshape(-1),
            column_sum(grad_query),
            column_sum(grad_values),
            column_sum(lax.dynamic_slice_in_dim(grad_proj_all, start, own, 1)),
            column_sum(lax.dynamic_slice_in_dim(grad_all, start, own, 1)),
            column_sum(grad_hidden),
        ]
    ).astype(BF16)
    piece = vectors_own.shape[0] // (2 * ctx)
    vector_part = pad_rows(
        jnp.pad(vectors_own.reshape(ctx, 2, 1, piece), [(0, 0)] * 3 + [(0, chunk - piece)])
    )
    parts = jnp.concatenate(
        [turned.reshape(ctx, 2, -1, chunk), down_part, dense_part, vector_part], axis=2
    )
    summed = sum_over_ctx(parts, turned_rows)
    at_down = wsh * turned_rows
    at_dense = at_down + down_part.shape[2]
    at_vector = at_dense + dense_part.shape[2]
    back = summed[:, :, :at_down].reshape(ctx, 2, wsh, turned_rows, chunk)
    back = back[:, :, :, : groups * fine].reshape(ctx, 2, wsh, groups, fine, chunk)

    def unturn(value, sections):
        shaped = value.astype(F32).reshape(ctx, 2, wsh, sections, -1, fine, chunk)
        return shaped.transpose(0, 1, 5, 3, 2, 4, 6).reshape(own, -1)

    up_groups = hidden_own // chunk
    grad_up_weight = unturn(back[:, :, :, :up_groups], 1)
    grad_qkv_weight = unturn(back[:, :, :, up_groups:], 3)
    grad_down_weight = uncut(summed[:, :, at_down:at_dense], width)
    grad_dense_weight = uncut(summed[:, :, at_dense:at_vector], width)
    sums = summed[:, :, at_vector, :piece].reshape(-1).astype(F32)
    (
        sum_gain_first, sum_shift_first, sum_gain_second, sum_shift_second,
        sum_query, sum_value, sum_dense, sum_down,
    ) = sums[: 8 * own].reshape(8, own)
    return (
        layer_out, input_grad, sum_gain_first, sum_shift_first, grad_qkv_weight, sum_query,
        sum_value, grad_dense_weight, sum_dense, sum_gain_second, sum_shift_second,
        grad_up_weight, sums[8 * own :], grad_down_weight, sum_down,
    )


def solution(mesh):
    rows, vec, tok = P("wsh", None), P("wsh"), P("wsh", "ctx", None)
    in_specs = (
        tok, P(), rows, vec, vec, rows, vec, vec, rows, vec, vec, vec, rows, vec, rows, vec, tok,
    )
    out_specs = (
        tok, tok, vec, vec, rows, vec, vec, rows, vec, vec, vec, rows, vec, rows, vec,
    )
    return jax.shard_map(body, mesh=mesh, in_specs=in_specs, out_specs=out_specs, check_vma=False)
```

```python
import functools

import jax
import jax.numpy as jnp
from jax import lax
from jax.experimental import pallas as pl
from jax.experimental.pallas import tpu as pltpu
from jax.sharding import PartitionSpec as P

HEADS = 16
EPS = 1e-05
LANES = 128
QUERY_TILE = 256
KEY_TILE = 512
FAR = -1e30
F32 = jnp.float32
BF16 = jnp.bfloat16


def norm_forward(values, gain_vec, shift_vec):
    row_mean = jnp.mean(values, axis=-1, keepdims=True)
    centered = values - row_mean
    variance = jnp.mean(centered * centered, axis=-1, keepdims=True)
    inverse = lax.rsqrt(variance + EPS)
    scaled = centered * inverse
    return (scaled * gain_vec + shift_vec, scaled, inverse)


def norm_backward(grad_out, scaled, inverse, gain_vec):
    grad_scaled = grad_out * gain_vec
    mean_grad = jnp.mean(grad_scaled, axis=-1, keepdims=True)
    mean_along = jnp.mean(grad_scaled * scaled, axis=-1, keepdims=True)
    grad_in = inverse * (grad_scaled - mean_grad - scaled * mean_along)
    return (grad_in, jnp.sum(grad_out * scaled, axis=0), jnp.sum(grad_out, axis=0))


def gelu_tanh(values):
    return jax.nn.gelu(values, approximate=True)


def dot(a, b, dims):
    return lax.dot_general(a, b, (dims, ((), ())), preferred_element_type=F32)


def column_sum(values):
    return jnp.sum(values.astype(F32), axis=0)


def slot_rows(order_ref, step, rows, first):
    slot = order_ref[step]
    src = slot // 2
    return src, pl.ds(pl.multiple_of(first + (slot % 2) * rows, 16), rows)


def split_heads(tile):
    lane = lax.broadcasted_iota(jnp.int32, tile.shape, 1)
    zero = jnp.zeros_like(tile)
    half = LANES // 2
    return (jnp.where(lane < half, tile, zero), jnp.where(lane >= half, tile, zero))


def load_sequence(query_block, half_tok, order_ref, packed_ref, q_s, k_s, v_s):
    first_key = 2 * query_block
    first_value = first_key + 2 * half_tok

    def load(step, _):
        src, rows = slot_rows(order_ref, step, query_block, 0)
        to = pl.ds(pl.multiple_of(step * query_block, 16), query_block)
        q_s[to, :] = packed_ref[src, rows, :]
        to = pl.ds(pl.multiple_of(step * half_tok, 16), half_tok)
        src, rows = slot_rows(order_ref, step, half_tok, first_key)
        k_s[to, :] = packed_ref[src, rows, :]
        src, rows = slot_rows(order_ref, step, half_tok, first_value)
        v_s[to, :] = packed_ref[src, rows, :]
        return 0

    lax.fori_loop(0, order_ref.shape[0], load, 0)


def transpose_into(to_ref, from_ref, key_tile):
    def turn(step, _):
        rows = pl.ds(pl.multiple_of(step * key_tile, key_tile), key_tile)
        to_ref[:, rows] = from_ref[rows, :].astype(F32).T.astype(BF16)
        return 0

    lax.fori_loop(0, from_ref.shape[0] // key_tile, turn, 0)


def tile_bias(key_pos_ref, keys, query_pos):
    distance = key_pos_ref[keys, :] - query_pos
    return jnp.where(distance <= 0.0, distance, FAR)


def forward_kernel(
    query_block, half_tok, query_tile, key_tile,
    order_ref, count_ref, slope_ref, packed_ref, query_pos_ref, key_pos_ref,
    context_ref, attended_ref, log_ref, q_s, k_s, v_s, vt_s,
):
    load_sequence(query_block, half_tok, order_ref, packed_ref, q_s, k_s, v_s)
    transpose_into(vt_s, v_s, key_tile)
    half = LANES // 2

    def query_step(qi, _):
        queries = pl.ds(pl.multiple_of(qi * query_tile, query_tile), query_tile)
        q_parts = split_heads(q_s[queries, :] * 0.125)
        query_pos = query_pos_ref[:, queries]

        def key_step(kj, carry):
            keys = pl.ds(pl.multiple_of(kj * key_tile, key_tile), key_tile)
            k_tile = k_s[keys, :]
            bias = tile_bias(key_pos_ref, keys, query_pos)
            out = []
            for h in range(2):
                top, total, acc = carry[h]
                scores = dot(k_tile, q_parts[h], ((1,), (1,))) + slope_ref[h] * bias
                new_top = jnp.maximum(top, jnp.max(scores, axis=0, keepdims=True))
                rescale = jnp.exp(top - new_top)
                weights = jnp.exp(scores - new_top)
                total = total * rescale + jnp.sum(weights, axis=0, keepdims=True)
                v_tile = vt_s[h * half : (h + 1) * half, keys]
                acc = acc * rescale + dot(v_tile, weights.astype(BF16), ((1,), (0,)))
                out.append((new_top, total, acc))
            return tuple(out)

        row = jnp.zeros((1, query_tile), F32)
        start = (row + FAR, row, jnp.zeros((half, query_tile), F32))
        ends = lax.fori_loop(0, count_ref[qi], key_step, (start, start))
        for h in range(2):
            top, total, acc = ends[h]
            attended_ref[h * half : (h + 1) * half, queries] = acc / total
            log_ref[h : h + 1, queries] = top + jnp.log(total)
        q_s[queries, :] = attended_ref[:, queries].T.astype(BF16)
        return 0

    lax.fori_loop(0, q_s.shape[0] // query_tile, query_step, 0)

    def put(step, _):
        src, rows = slot_rows(order_ref, step, query_block, 0)
        at = pl.ds(pl.multiple_of(step * query_block, 16), query_block)
        context_ref[src, rows, :] = q_s[at, :]
        return 0

    lax.fori_loop(0, order_ref.shape[0], put, 0)


def backward_kernel(
    query_block, half_tok, query_tile, key_tile,
    order_ref, count_ref, slope_ref, packed_ref, query_pos_ref, key_pos_ref,
    attended_ref, log_ref, grad_ref,
    out_ref, q_s, k_s, v_s, kt_s, g_s, gk_s, gv_s,
):
    load_sequence(query_block, half_tok, order_ref, packed_ref, q_s, k_s, v_s)
    transpose_into(kt_s, k_s, key_tile)
    half = LANES // 2

    def load(step, _):
        src, rows = slot_rows(order_ref, step, query_block, 0)
        at = pl.ds(pl.multiple_of(step * query_block, 16), query_block)
        g_s[at, :] = grad_ref[src, rows, :]
        return 0

    lax.fori_loop(0, order_ref.shape[0], load, 0)
    gk_s[...] = jnp.zeros_like(gk_s)
    gv_s[...] = jnp.zeros_like(gv_s)

    def query_step(qi, _):
        queries = pl.ds(pl.multiple_of(qi * query_tile, query_tile), query_tile)
        q_parts = split_heads(q_s[queries, :] * 0.125)
        g_tile = g_s[queries, :]
        g_parts = split_heads(g_tile)
        along = g_tile.astype(F32).T * attended_ref[:, queries]
        deltas = [
            jnp.sum(along[h * half : (h + 1) * half], axis=0, keepdims=True) for h in range(2)
        ]
        query_pos = query_pos_ref[:, queries]

        def key_step(kj, carry):
            keys = pl.ds(pl.multiple_of(kj * key_tile, key_tile), key_tile)
            k_tile, v_tile = k_s[keys, :], v_s[keys, :]
            bias = tile_bias(key_pos_ref, keys, query_pos)
            out = []
            add_k, add_v = gk_s[keys, :], gv_s[keys, :]
            for h in range(2):
                scores = dot(k_tile, q_parts[h], ((1,), (1,))) + slope_ref[h] * bias
                weights = jnp.exp(scores - log_ref[h : h + 1, queries])
                grads = dot(v_tile, g_parts[h], ((1,), (1,)))
                raw = (weights * (grads - deltas[h])).astype(BF16)
                add_v = add_v + dot(weights.astype(BF16), g_parts[h], ((1,), (0,)))
                add_k = add_k + dot(raw, q_parts[h], ((1,), (0,)))
                out.append(carry[h] + dot(kt_s[h * half : (h + 1) * half, keys], raw, ((1,), (0,))))
            gk_s[keys, :] = add_k
            gv_s[keys, :] = add_v
            return tuple(out)

        start = jnp.zeros((half, query_tile), F32)
        ends = lax.fori_loop(0, count_ref[qi], key_step, (start, start))
        grad_q = jnp.concatenate(ends, axis=0) * 0.125
        q_s[queries, :] = grad_q.T.astype(BF16)
        return 0

    lax.fori_loop(0, q_s.shape[0] // query_tile, query_step, 0)
    first_key = 2 * query_block
    first_value = first_key + 2 * half_tok

    def put(step, _):
        src, rows = slot_rows(order_ref, step, query_block, 0)
        at = pl.ds(pl.multiple_of(step * query_block, 16), query_block)
        out_ref[src, rows, :] = q_s[at, :]
        at = pl.ds(pl.multiple_of(step * half_tok, 16), half_tok)
        src, rows = slot_rows(order_ref, step, half_tok, first_key)
        out_ref[src, rows, :] = gk_s[at, :].astype(BF16)
        src, rows = slot_rows(order_ref, step, half_tok, first_value)
        out_ref[src, rows, :] = gv_s[at, :].astype(BF16)
        return 0

    lax.fori_loop(0, order_ref.shape[0], put, 0)


def call_local(kernel, outs, scratch, flops, *args):
    smem = pl.BlockSpec(memory_space=pltpu.SMEM)
    vmem = pl.BlockSpec(memory_space=pltpu.VMEM)
    return pl.pallas_call(
        kernel,
        out_shape=outs,
        in_specs=[smem] * 3 + [vmem] * (len(args) - 3),
        out_specs=[vmem] * len(outs),
        scratch_shapes=scratch,
        cost_estimate=pl.CostEstimate(flops=flops, bytes_accessed=6_000_000, transcendentals=flops // 256),
        compiler_params=pltpu.CompilerParams(vmem_limit_bytes=48 * 1024 * 1024),
    )(*args)


def add_low(a, b):
    return (a.astype(F32) + b.astype(F32)).astype(BF16)


def ring_place(index, count):
    odd = index % 2
    return (1 - odd) * (index // 2) + odd * (count - 1 - index // 2)


def ring_index(place, count):
    late = place // (count // 2)
    return (1 - late) * 2 * place + late * (2 * (count - 1 - place) + 1)


def sum_kernel(
    count, peers, turned, part_ref, out_ref, held, mine,
    send_sem, recv_sem, turn_send, turn_recv, back_send, back_recv,
):
    place = ring_place(lax.axis_index("ctx"), count)
    me = lax.axis_index("wsh")
    sides = (
        ring_index((place + 1) % count, count), ring_index((place + count - 1) % count, count)
    )
    barrier = pltpu.get_barrier_semaphore()
    for side in sides:
        pl.semaphore_signal(
            barrier, inc=1, device_id={"ctx": side}, device_id_type=pl.DeviceIdType.MESH
        )
    for step in range(1, peers):
        pl.semaphore_signal(
            barrier, inc=1, device_id={"wsh": (me + step) % peers},
            device_id_type=pl.DeviceIdType.MESH,
        )
    pl.semaphore_wait(barrier, 1 + peers)

    def chunk(way, back):
        return (place + count - back) % count if way == 0 else (place + back) % count

    def send(way, step, src):
        return pltpu.make_async_remote_copy(
            src_ref=src, dst_ref=held.at[step, way],
            send_sem=send_sem.at[step, way], recv_sem=recv_sem.at[step, way],
            device_id={"ctx": sides[way]}, device_id_type=pl.DeviceIdType.MESH,
        )

    for way in range(2):
        send(way, 0, part_ref.at[chunk(way, 1), way]).start()

    def reduce_step(step, _):
        for way in range(2):
            here = held.at[step - 1, way]
            send(way, step - 1, here).wait_recv()
            here[...] = add_low(here[...], part_ref[chunk(way, step + 1), way])
            send(way, step, here).start()
        return 0

    lax.fori_loop(1, count - 1, reduce_step, 0)
    for way in range(2):
        last = held.at[count - 2, way]
        send(way, count - 2, last).wait_recv()
        mine[way] = add_low(last[...], part_ref[place, way])

    def turn(step):
        peer = (me + step) % peers
        return pltpu.make_async_remote_copy(
            src_ref=mine.at[:, pl.ds(pl.multiple_of(peer * turned, 16), turned), :],
            dst_ref=out_ref.at[place, :, pl.ds(pl.multiple_of(me * turned, 16), turned), :],
            send_sem=turn_send.at[step - 1], recv_sem=turn_recv.at[step - 1],
            device_id={"wsh": peer}, device_id_type=pl.DeviceIdType.MESH,
        )

    for step in range(1, peers):
        turn(step).start()
    kept = pl.ds(pl.multiple_of(me * turned, 16), turned)
    out_ref[place, :, kept, :] = mine[:, kept, :]
    out_ref[place, :, peers * turned :, :] = mine[:, peers * turned :, :]
    for step in range(1, peers):
        turn(step).wait_recv()

    def pass_on(way, step):
        here = out_ref.at[chunk(way, step), way]
        return pltpu.make_async_remote_copy(
            src_ref=here, dst_ref=here,
            send_sem=back_send.at[step, way], recv_sem=back_recv.at[step, way],
            device_id={"ctx": sides[way]}, device_id_type=pl.DeviceIdType.MESH,
        )

    for way in range(2):
        pass_on(way, 0).start()

    def gather_step(step, _):
        for way in range(2):
            pass_on(way, step - 1).wait_recv()
            pass_on(way, step).start()
        return 0

    lax.fori_loop(1, count - 1, gather_step, 0)
    for way in range(2):
        pass_on(way, count - 2).wait_recv()
    for step in range(1, peers):
        turn(step).wait_send()

    def drain(step, _):
        for way in range(2):
            send(way, step, held.at[step, way]).wait_send()
            pass_on(way, step).wait_send()
        return 0

    lax.fori_loop(0, count - 1, drain, 0)


def sum_over_ctx(parts, turned):
    count, _, rows, width = parts.shape
    peers = lax.axis_size("wsh")
    sems = pltpu.SemaphoreType.DMA((count - 1, 2))
    turn_sems = pltpu.SemaphoreType.DMA((peers - 1,))
    return pl.pallas_call(
        functools.partial(sum_kernel, count, peers, turned),
        out_shape=jax.ShapeDtypeStruct(parts.shape, BF16),
        in_specs=[pl.BlockSpec(memory_space=pltpu.VMEM)],
        out_specs=pl.BlockSpec(memory_space=pltpu.VMEM),
        scratch_shapes=[
            pltpu.VMEM((count - 1, 2, rows, width), BF16),
            pltpu.VMEM((2, rows, width), BF16),
            sems, sems, turn_sems, turn_sems, sems, sems,
        ],
        cost_estimate=pl.CostEstimate(flops=parts.size, bytes_accessed=300_000_000, transcendentals=0),
        compiler_params=pltpu.CompilerParams(
            collective_id=0, has_side_effects=True, vmem_limit_bytes=40 * 1024 * 1024
        ),
    )(parts)


def body(
    tokens, block_map, positions, norm_gain_one, norm_shift_one, qkv_weight, query_bias,
    value_bias, dense_weight, dense_bias, norm_gain_two, norm_shift_two, up_weight, up_bias,
    down_weight, down_bias, cotangent,
):
    width = tokens.shape[2]
    count_tok = tokens.shape[1]
    half_tok = count_tok // 2
    ctx = lax.axis_size("ctx")
    wsh = lax.axis_size("wsh")
    blocks = 2 * ctx
    length = ctx * count_tok
    own = width // wsh
    pairs = own // LANES
    units = wsh * pairs
    share = max(1, ctx // units)
    query_block = half_tok // share
    query_count = length // share
    query_tile = min(QUERY_TILE, query_count)
    key_tile = min(KEY_TILE, length)
    all_tok = wsh * count_tok

    def gather(value):
        return lax.all_gather(value, "wsh", axis=0, tiled=True)

    def scatter(value):
        return lax.psum_scatter(value, "wsh", scatter_dimension=0, tiled=True)

    def swap_ctx(value):
        return lax.all_to_all(value, "ctx", split_axis=0, concat_axis=0, tiled=True)

    vectors = jnp.stack(
        [norm_gain_one, norm_shift_one, dense_bias, norm_gain_two, norm_shift_two, down_bias]
    )
    vectors = lax.all_gather(vectors, "wsh", axis=1, tiled=True).astype(F32)
    gain_first, shift_first, dense_shift, gain_second, shift_second, down_shift = vectors
    all_pos = gather(positions)
    qkv_own = lax.all_to_all(
        qkv_weight.reshape(own, 3, wsh, own), "wsh", split_axis=2, concat_axis=0, tiled=True
    ).reshape(width, 3 * own)
    hidden_own = up_weight.shape[1] // wsh
    unit = lax.axis_index("ctx") // share
    part = lax.axis_index("ctx") % share
    seq_pos = lax.dynamic_index_in_dim(all_pos, unit // pairs, 0, keepdims=False)
    stored = block_map.reshape(-1)
    ids = jnp.arange(blocks, dtype=jnp.int32)
    order = jnp.sum(jnp.where(stored[None, :] == ids[:, None], ids[None, :], 0), axis=1)
    query_pos = lax.dynamic_index_in_dim(
        seq_pos.reshape(blocks, share, query_block), part, 1, keepdims=False
    ).reshape(query_count)
    last_pos = query_pos.reshape(-1, query_tile)[:, -1]
    first_pos = seq_pos.reshape(-1, key_tile)[:, 0]
    counts = jnp.sum((first_pos[None, :] <= last_pos[:, None]).astype(jnp.int32), axis=1)
    head_ids = lax.axis_index("wsh") * (HEADS // wsh) + (unit % pairs) * 2 + jnp.arange(2)
    slopes = 2.0 ** (-8.0 * (head_ids.astype(F32) + 1.0) / HEADS)
    query_row = query_pos.astype(F32).reshape(1, query_count)
    key_column = seq_pos.astype(F32).reshape(length, 1)

    def to_query_units(value):
        shaped = value.reshape(wsh, 2, share, query_block, pairs, LANES)
        return shaped.transpose(0, 4, 2, 1, 3, 5).reshape(ctx, 2 * query_block, LANES)

    def from_query_units(value):
        shaped = value.reshape(wsh, pairs, share, 2, query_block, LANES)
        return shaped.transpose(0, 3, 2, 4, 1, 5).reshape(all_tok, own)

    def to_key_units(value):
        shaped = value.reshape(wsh, count_tok, pairs, LANES).transpose(0, 2, 1, 3)
        shaped = jnp.broadcast_to(shaped[:, :, None], (wsh, pairs, share, count_tok, LANES))
        return shaped.reshape(ctx, count_tok, LANES)

    def from_key_units(value):
        shaped = value.reshape(wsh, pairs, share, count_tok, LANES)
        if share == 1:
            shaped = shaped[:, :, 0]
        else:
            shaped = jnp.sum(shaped.astype(F32), axis=2).astype(BF16)
        return shaped.transpose(0, 2, 1, 3).reshape(all_tok, own)

    inputs = tokens[0].astype(F32)
    normed, scaled_first, inverse_first = norm_forward(inputs, gain_first, shift_first)
    normed_all = gather(normed.astype(BF16))
    grad_all = gather(cotangent[0])
    mixed = jnp.dot(normed_all, qkv_own, preferred_element_type=F32)
    query = (mixed[:, :own] + query_bias.astype(F32)).astype(BF16)
    keys = mixed[:, own : 2 * own].astype(BF16)
    values = (mixed[:, 2 * own :] + value_bias.astype(F32)).astype(BF16)
    packed = swap_ctx(
        jnp.concatenate([to_query_units(query), to_key_units(keys), to_key_units(values)], axis=1)
    )
    packed, up_late = lax.optimization_barrier((packed, up_weight))
    up_own = lax.all_to_all(
        up_late.reshape(own, wsh, hidden_own), "wsh", split_axis=1, concat_axis=0, tiled=True
    ).reshape(width, hidden_own)
    sizes = (query_block, half_tok, query_tile, key_tile)
    flops = 4 * query_count * length * LANES
    context_units, attended, logs = call_local(
        functools.partial(forward_kernel, *sizes),
        [
            jax.ShapeDtypeStruct((ctx, 2 * query_block, LANES), BF16),
            jax.ShapeDtypeStruct((LANES, query_count), F32),
            jax.ShapeDtypeStruct((2, query_count), F32),
        ],
        [
            pltpu.VMEM((query_count, LANES), BF16),
            pltpu.VMEM((length, LANES), BF16),
            pltpu.VMEM((length, LANES), BF16),
            pltpu.VMEM((LANES, length), BF16),
        ],
        flops,
        order, counts, slopes, packed, query_row, key_column,
    )
    context_units, up_own = lax.optimization_barrier((context_units, up_own))
    context = from_query_units(swap_ctx(context_units))
    projected = scatter(jnp.dot(context, dense_weight, preferred_element_type=F32).astype(BF16))
    middle = inputs + projected.astype(F32) + dense_shift
    normed_two, scaled_second, inverse_second = norm_forward(middle, gain_second, shift_second)
    normed_two_all = gather(normed_two.astype(BF16))
    hidden = jnp.dot(normed_two_all, up_own, preferred_element_type=F32) + up_bias.astype(F32)
    activated, gelu_back = jax.vjp(gelu_tanh, hidden)
    active = activated.astype(BF16)
    branch_part = jnp.dot(active, down_weight, preferred_element_type=F32).astype(BF16)

    grad_active = dot(grad_all, down_weight, ((1,), (1,)))
    grad_hidden = gelu_back(grad_active)[0].astype(BF16)
    grad_normed_two = scatter(dot(grad_hidden, up_own, ((1,), (1,))).astype(BF16)).astype(F32)
    grad_middle_part, grad_gain_second, grad_shift_second = norm_backward(
        grad_normed_two, scaled_second, inverse_second, gain_second
    )
    grad_middle = cotangent[0].astype(F32) + grad_middle_part
    grad_proj_all = gather(grad_middle.astype(BF16))
    branch_part, grad_proj_all = lax.optimization_barrier((branch_part, grad_proj_all))
    branch = scatter(branch_part)
    layer_out = (middle + branch.astype(F32) + down_shift).astype(BF16)[None]
    grad_context = dot(grad_proj_all, dense_weight, ((1,), (1,))).astype(BF16)
    grad_units = swap_ctx(to_query_units(grad_context))
    (grad_packed,) = call_local(
        functools.partial(backward_kernel, *sizes),
        [jax.ShapeDtypeStruct(packed.shape, BF16)],
        [
            pltpu.VMEM((query_count, LANES), BF16),
            pltpu.VMEM((length, LANES), BF16),
            pltpu.VMEM((length, LANES), BF16),
            pltpu.VMEM((LANES, length), BF16),
            pltpu.VMEM((query_count, LANES), BF16),
            pltpu.VMEM((length, LANES), F32),
            pltpu.VMEM((length, LANES), F32),
        ],
        flops * 5 // 2,
        order, counts, slopes, packed, query_row, key_column, attended, logs, grad_units,
    )
    grad_packed = swap_ctx(grad_packed)
    first_key = 2 * query_block
    first_value = first_key + count_tok
    grad_query = from_query_units(grad_packed[:, :first_key])
    grad_keys = from_key_units(grad_packed[:, first_key:first_value])
    grad_values = from_key_units(grad_packed[:, first_value:])
    grad_mixed = jnp.concatenate([grad_query, grad_keys, grad_values], axis=1)
    grad_normed = scatter(dot(grad_mixed, qkv_own, ((1,), (1,))).astype(BF16)).astype(F32)
    grad_input_part, grad_gain_first, grad_shift_first = norm_backward(
        grad_normed, scaled_first, inverse_first, gain_first
    )
    input_grad = (grad_middle + grad_input_part).astype(BF16)[None]

    chunk = width

    def cut(value):
        shaped = value.astype(BF16).reshape(ctx, 2, -1, value.shape[1] // chunk, chunk)
        return shaped.transpose(0, 1, 3, 2, 4).reshape(ctx, 2, -1, chunk)

    def uncut(value, columns):
        shaped = value.astype(F32).reshape(ctx, 2, columns // chunk, -1, chunk)
        return shaped.transpose(0, 1, 3, 2, 4).reshape(-1, columns)

    def pad_rows(value):
        return jnp.pad(value, [(0, 0)] * (value.ndim - 2) + [(0, -value.shape[-2] % 16), (0, 0)])

    up_groups = hidden_own // chunk
    groups = up_groups + 1
    fine = own // (2 * ctx)
    turned = jnp.concatenate(
        [
            dot(normed_two_all, grad_hidden, ((0,), (0,))).astype(BF16),
            jnp.pad(
                dot(normed_all, grad_mixed, ((0,), (0,))).astype(BF16),
                ((0, 0), (0, chunk - 3 * own)),
            ),
        ],
        axis=1,
    ).reshape(wsh, ctx, 2, fine, groups, chunk)
    turned = pad_rows(
        turned.transpose(1, 2, 0, 4, 3, 5).reshape(ctx, 2, wsh, groups * fine, chunk)
    )
    turned_rows = turned.shape[3]
    down_part = cut(dot(active, grad_all, ((0,), (0,))))
    dense_part = cut(dot(context, grad_proj_all, ((0,), (0,))))
    norms = jnp.stack([grad_gain_first, grad_shift_first, grad_gain_second, grad_shift_second])
    norms = lax.psum_scatter(norms, "wsh", scatter_dimension=1, tiled=True)
    start = lax.axis_index("wsh") * own
    vectors_own = jnp.concatenate(
        [
            norms.reshape(-1),
            column_sum(grad_query),
            column_sum(grad_values),
            column_sum(lax.dynamic_slice_in_dim(grad_proj_all, start, own, 1)),
            column_sum(lax.dynamic_slice_in_dim(grad_all, start, own, 1)),
            column_sum(grad_hidden),
        ]
    ).astype(BF16)
    piece = vectors_own.shape[0] // (2 * ctx)
    vector_part = pad_rows(
        jnp.pad(vectors_own.reshape(ctx, 2, 1, piece), [(0, 0)] * 3 + [(0, chunk - piece)])
    )
    parts = jnp.concatenate(
        [turned.reshape(ctx, 2, -1, chunk), down_part, dense_part, vector_part], axis=2
    )
    summed = sum_over_ctx(parts, turned_rows)
    at_down = wsh * turned_rows
    at_dense = at_down + down_part.shape[2]
    at_vector = at_dense + dense_part.shape[2]
    back = summed[:, :, :at_down].reshape(ctx, 2, wsh, turned_rows, chunk)
    back = back[:, :, :, : groups * fine].reshape(ctx, 2, wsh, groups, fine, chunk)

    up_back = back[:, :, :, :up_groups].astype(F32)
    grad_up_weight = up_back.transpose(0, 1, 4, 2, 3, 5).reshape(own, -1)
    qkv_back = back[:, :, :, up_groups, :, : 3 * own].astype(F32)
    qkv_back = qkv_back.reshape(ctx, 2, wsh, fine, 3, own)
    grad_qkv_weight = qkv_back.transpose(0, 1, 3, 4, 2, 5).reshape(own, -1)
    grad_down_weight = uncut(summed[:, :, at_down:at_dense], width)
    grad_dense_weight = uncut(summed[:, :, at_dense:at_vector], width)
    sums = summed[:, :, at_vector, :piece].reshape(-1).astype(F32)
    (
        sum_gain_first, sum_shift_first, sum_gain_second, sum_shift_second,
        sum_query, sum_value, sum_dense, sum_down,
    ) = sums[: 8 * own].reshape(8, own)
    return (
        layer_out, input_grad, sum_gain_first, sum_shift_first, grad_qkv_weight, sum_query,
        sum_value, grad_dense_weight, sum_dense, sum_gain_second, sum_shift_second,
        grad_up_weight, sums[8 * own :], grad_down_weight, sum_down,
    )


def solution(mesh):
    rows, vec, tok = P("wsh", None), P("wsh"), P("wsh", "ctx", None)
    in_specs = (
        tok, P(), rows, vec, vec, rows, vec, vec, rows, vec, vec, vec, rows, vec, rows, vec, tok,
    )
    out_specs = (
        tok, tok, vec, vec, rows, vec, vec, rows, vec, vec, vec, rows, vec, rows, vec,
    )
    return jax.shard_map(body, mesh=mesh, in_specs=in_specs, out_specs=out_specs, check_vma=False)
```
